256 devices in a mesh: row: 16 (over y, z_lo), col: 16 (over x, z_hi, core).
Axes of the slice: x: 4, y: 4, z: 8 (z_hi: 2, z_lo: 4; z = z_hi * 4 + z_lo), core: 2. Of those that a mesh axis runs over, the one named last changes fastest.
Arguments:
- a_vals: bfloat16 [320, 80, 4096], P('row', 'col'), may hold values from -0.3125 to 0.3125
- a_cols: int32 [320, 80], P('row', 'col'), may hold values from 0 to 319, as said below
- a_count: int32 [320, 16], P('row', 'col'), may hold values from 3 to 5, as said below
- p_vals: bfloat16 [320, 64, 2048], P('row', None, 'col'), may hold values from -0.6015625 to 0.6015625
- p_mask: int32 [320, 16], P('row', 'col'), may hold values 0 or 1
Outputs:
- coarse: float32 [2048, 2048], P('row', 'col')
The draws below stay inside these ranges and needn't reach their ends.
Inputs may be any that keep to these rules, and one draw needn't show every extreme that they name: a_cols[i, j] lies in column range j // 5, that is from (j // 5) * 20 to (j // 5) * 20 + 19; entries of slots that are not live are ignored. `a_count`: in the column range that holds the row's own index (range i // 20) the count is 4 to 5 and 5 is reached; in every other range it is 3 to 4 and 4 is reached.
All inputs are finite; a program needn't handle non-finite values. No bound on the sum of `p_mask` on one device may be relied on, other than what follows from the above.
Results may differ from the reference program's by a relative error of at most 0.0029.
Values may be sent and summed in bfloat16 or wider, within the bound.
No kernel may reach another device: no remote copies, remote signals or barrier semaphores. Data moves between devices by JAX's collectives and lax.ppermute only.
A program may use at most 128 MiB of HBM per device.

```python
import jax
import jax.numpy as jnp
from jax import lax

BR = 64
BC = 128
FB = 20
SA = 5
SO = 4
NF = 320
NC = 16
N_COL = 16


def draw_a_cols(key, part):
    key = jax.random.fold_in(key, 11)
    offset = jax.random.randint(key, (NF, N_COL * SA), 0, FB)
    ranges = jnp.arange(N_COL * SA, dtype=jnp.int32) // SA
    return (ranges[None, :] * FB + offset).astype(jnp.int32)


def draw_a_count(key, part):
    key = jax.random.fold_in(key, 23)
    first_key, second_key = jax.random.split(key)
    others = jax.random.randint(first_key, (NF, N_COL), SO - 1, SO + 1)
    own_range = jax.random.randint(second_key, (NF, N_COL), SO, SA + 1)
    diagonal = (jnp.arange(NF, dtype=jnp.int32) // FB)[:, None] == jnp.arange(N_COL, dtype=jnp.int32)[None, :]
    counts = jnp.where(diagonal, own_range, others)
    counts = counts.at[0, 0].set(SA).at[0, 1].set(SO)
    return counts.astype(jnp.int32)


def with_ends(array, own_key, low, high):
    longest = array.shape.index(max(array.shape))
    spots = []
    for shift in (0, 1):
        where = [jax.random.randint(jax.random.fold_in(own_key, axis), (), 0, length) for axis, length in enumerate(array.shape)]
        where[longest] = (where[longest] + shift) % array.shape[longest]
        spots.append(tuple(where))
    return array.at[spots[0]].set(low).at[spots[1]].set(high)


def block_levels(key, dims, cuts, least, high):
    gain = 1.0
    for axis_at, parts in cuts:
        draws = jax.random.uniform(jax.random.fold_in(jax.random.fold_in(key, 6), axis_at), (parts,), jnp.float32, least / len(cuts), high / len(cuts))
        gain = gain * jnp.repeat(jnp.exp(draws), dims[axis_at] // parts).reshape((-1,) + (1,) * (len(dims) - 1 - axis_at))
    return gain


def centred(stream_key, extent, scale, reach, cuts=(), kind=jnp.bfloat16):
    values = scale * jax.random.normal(stream_key, extent, jnp.float32)
    if cuts:
        values = values * block_levels(stream_key, extent, cuts, -0.22, 0.18)
    return jnp.clip(values, -reach, reach).astype(kind)


def setup_inputs(seed: int = 0) -> dict:
    key_of = jax.random.split(jax.random.key(seed), 6)
    return {
        "a_vals": centred(key_of[0], (NF, N_COL * SA, BR * BR), (BR * SA) ** -0.5, 0.3125, ((0, 16), (1, 16))),
        "a_cols": draw_a_cols(jax.random.fold_in(key_of[5], 71), 0),
        "a_count": draw_a_count(jax.random.fold_in(key_of[5], 71), 0),
        "p_vals": centred(key_of[3], (NF, BR, NC * BC), (1.2 * (NF * BR) ** -0.25), 0.6015625, ((0, 16), (2, 16))),
        "p_mask": with_ends((jax.random.randint(key_of[4], (NF, NC), 0, 2) < 1).astype(jnp.int32), jax.random.fold_in(key_of[4], 1), 0, 1),
    }


def reference(a_vals, a_cols, a_count, p_vals, p_mask):
    per = a_cols.shape[1] // N_COL
    slot_pos = jnp.arange(a_cols.shape[1], dtype=jnp.int32) % per
    live = slot_pos[None, :] < jnp.repeat(a_count, per, axis=1)
    masked = jnp.where(live[:, :, None], a_vals, jnp.zeros_like(a_vals))
    fine_blocks = p_vals.shape[0]
    width = p_vals.shape[2] // N_COL
    p_live = (p_vals.reshape(fine_blocks, BR, N_COL, width) * p_mask[:, None, :, None].astype(p_vals.dtype)).reshape(fine_blocks, BR, N_COL * width)

    def one_row(item):
        values, columns = item
        blocks = values.reshape(values.shape[0], BR, BR).astype(jnp.float32)
        picked = p_live[columns.astype(jnp.int32)].astype(jnp.float32)
        return jnp.einsum("tab,tbc->ac", blocks, picked).astype(jnp.bfloat16)

    prolonged = lax.map(one_row, (masked, a_cols))
    flat_p = p_live.reshape(fine_blocks * BR, N_COL * width)
    flat_ap = prolonged.reshape(fine_blocks * BR, N_COL * width)
    return jnp.dot(flat_p.T, flat_ap, preferred_element_type=jnp.float32)
```

```python
import jax
import jax.numpy as jnp
from jax import lax
from jax.experimental import pallas as pl
from jax.experimental.pallas import tpu as pltpu
from jax.sharding import PartitionSpec as P

BR = 64
AXES = ("row", "col")


def flat(y, z, x, h, c):
    return ((y * 4 + z) * 4 + x) * 4 + h * 2 + c


PLACES = [
    (y, z, x, h, c)
    for y in range(4)
    for z in range(4)
    for x in range(4)
    for h in range(2)
    for c in range(2)
]


def move(array, target):
    pairs = []
    for place in PLACES:
        to = target(*place)
        if to is not None:
            pairs.append((flat(*place), flat(*to)))
    return lax.ppermute(array, AXES, pairs)


def shift_y(k):
    return lambda y, z, x, h, c: ((y + k) % 4, z, x, h, c)


def shift_x(k):
    return lambda y, z, x, h, c: (y, z, (x + k) % 4, h, c)


def shift_z(k):
    return lambda y, z, x, h, c: (y, (z + k) % 4, x, h, c)


def flip_h(y, z, x, h, c):
    return (y, z, x, 1 - h, c)


def flip_c(y, z, x, h, c):
    return (y, z, x, h, 1 - c)


def swap_zc(y, z, x, h, c):
    return (y, (z // 2) * 2 + c, x, h, z % 2)


def ring(array, shift):
    half = array.shape[0] // 2
    before = move(array, shift(1))
    after = move(array, shift(3))
    first = move(before[:half], shift(1))
    second = move(after[half:], shift(3))
    return [array, before, after, first, second]


def apply_kernel(idx, place, *refs):
    p_refs = refs[:20]
    a_refs = refs[20:30]
    a5_ref = refs[30]
    mine, other = refs[31:33]
    panel, left, sems = refs[33:]
    y, z, x, h, c = (place[i] for i in range(5))
    copies = []

    def start(src, dst):
        copy = pltpu.make_async_copy(src, dst, sems.at[len(copies)])
        copy.start()
        copies.append(copy)

    for f in range(2):
        for k, (ref, rows, at) in enumerate(
            zip(a_refs[5 * f : 5 * f + 5], (1280, 1280, 1280, 640, 640), (0, 0, 0, 0, 640))
        ):
            slot = (0, 1, 3, 2, 2)[k] * 2 + f
            start(ref, left.at[slot, pl.ds(at, rows)])
    for d in range(4):
        source = lax.rem(z + 4 - d, 4)
        j1, l0 = source // 2, lax.rem(source, 2)
        side = lax.rem(l0 + c, 2)
        for k, (ref, rows, at) in enumerate(
            zip(p_refs[5 * d : 5 * d + 5], (1280, 1280, 1280, 640, 640), (0, 0, 0, 0, 640))
        ):
            jx = lax.rem(y + 4 - (0, 1, 3, 2, 2)[k], 4)
            start(ref, panel.at[side, pl.ds(pl.multiple_of((jx * 2 + j1) * 1280 + at, 640), rows)])
    for copy in copies:
        copy.wait()

    own = lax.rem(x + 4 - y, 4) * 2 + lax.rem(h + z // 2, 2)

    def block(off):
        rows = pl.ds(pl.multiple_of(off, BR), BR)
        return jnp.concatenate([panel[0, rows, :], panel[1, rows, :]], axis=1)

    @pl.loop(0, 20)
    def _(t):
        rows = pl.ds(pl.multiple_of(t * BR, BR), BR)
        total = jnp.dot(
            a5_ref[rows, :], block(idx[(own * 20 + t) * 5 + 4]), preferred_element_type=jnp.float32
        )
        for slot in range(8):
            at = (slot * 20 + t) * 5
            right = jnp.concatenate([block(idx[at + s]) for s in range(4)], axis=0)
            total += jnp.dot(left[slot, rows, :], right, preferred_element_type=jnp.float32)
        mine[rows, :] = total[:, :128]
        other[rows, :] = total[:, 128:]


def apply_panel(idx, place, p_pieces, a_pieces, a5):
    anywhere = pl.BlockSpec(memory_space=pl.ANY)
    inside = pl.BlockSpec(memory_space=pltpu.VMEM)
    out = jax.ShapeDtypeStruct((1280, 128), jnp.float32)
    return pl.pallas_call(
        apply_kernel,
        out_shape=(out, out),
        grid_spec=pltpu.PrefetchScalarGridSpec(
            num_scalar_prefetch=2,
            grid=(),
            in_specs=[anywhere] * 30 + [inside],
            out_specs=(inside, inside),
            scratch_shapes=[
                pltpu.VMEM((2, 8 * 1280, 128), jnp.bfloat16),
                pltpu.VMEM((8, 1280, 256), jnp.bfloat16),
                pltpu.SemaphoreType.DMA((30,)),
            ],
        ),
        compiler_params=pltpu.CompilerParams(vmem_limit_bytes=40 * 2**20),
        cost_estimate=pl.CostEstimate(
            flops=2 * 1280 * 2048 * 256, bytes_accessed=12 * 2**20, transcendentals=0
        ),
        name="apply_panel",
    )(idx, place, *p_pieces, *a_pieces, a5)


def project_kernel(place, *refs):
    t_refs = refs[:10]
    prol = refs[10]
    outs = refs[11:15]
    left, sems = refs[15:]
    y, z, x, h, c = (place[i] for i in range(5))
    copies = []
    for f in range(2):
        k1 = lax.rem(h + f, 2)
        for k, (rows, at) in enumerate(((128, 0), (128, 0), (128, 0), (64, 0), (64, 64))):
            m = lax.rem(x + 8 - (0, 1, 3, 2, 2)[k] - y, 4)
            copy = pltpu.make_async_copy(
                t_refs[5 * f + k], left.at[m, k1, pl.ds(at, rows)], sems.at[len(copies)]
            )
            copy.start()
            copies.append(copy)
    for copy in copies:
        copy.wait()
    for m in range(4):
        got = jnp.dot(
            left[m].reshape(256, 1280), prol[...], preferred_element_type=jnp.float32
        )
        outs[m][...] = got


def project(place, t_pieces, prol):
    anywhere = pl.BlockSpec(memory_space=pl.ANY)
    inside = pl.BlockSpec(memory_space=pltpu.VMEM)
    out = jax.ShapeDtypeStruct((256, 256), jnp.float32)
    return pl.pallas_call(
        project_kernel,
        out_shape=(out,) * 4,
        grid_spec=pltpu.PrefetchScalarGridSpec(
            num_scalar_prefetch=1,
            grid=(),
            in_specs=[anywhere] * 10 + [inside],
            out_specs=(inside,) * 4,
            scratch_shapes=[
                pltpu.VMEM((4, 2, 128, 1280), jnp.bfloat16),
                pltpu.SemaphoreType.DMA((10,)),
            ],
        ),
        compiler_params=pltpu.CompilerParams(vmem_limit_bytes=32 * 2**20),
        cost_estimate=pl.CostEstimate(
            flops=2 * 1280 * 1024 * 256, bytes_accessed=4 * 2**20, transcendentals=0
        ),
        name="project",
    )(place, *t_pieces, prol)


def per_device(a_vals, a_cols, a_count, p_vals, p_mask):
    row, col = lax.axis_index("row"), lax.axis_index("col")
    y, z = row // 4, row % 4
    x, h, c = col // 4, (col // 2) % 2, col % 2
    place = jnp.stack([y, z, x, h, c]).astype(jnp.int32)

    p_live = p_vals * p_mask[:, :, None].astype(jnp.bfloat16)
    p_flat = p_live.reshape(1280, 128)
    p_own = move(p_flat, swap_zc)
    p_pieces = []
    for d in range(4):
        piece = p_own if d == 0 else move(p_own, shift_z(d))
        p_pieces += ring(piece, shift_y)

    live = jnp.arange(5, dtype=jnp.int32)[None, :] < a_count
    masked = jnp.where(live[:, :, None], a_vals, jnp.zeros_like(a_vals))
    slots = masked.reshape(20, 5, BR, BR)
    four = slots[:, :4].transpose(0, 2, 1, 3).reshape(1280, 256)
    five = slots[:, 4].reshape(1280, BR)
    a_pieces = ring(four, shift_x) + ring(move(four, flip_h), shift_x)

    def from_own(step):
        def target(y, z, x, h, c):
            if x != y or c != z % 2:
                return None
            return step(y, z, x, h, c)

        return target

    def across(y, z, x, h, c):
        return (y, z, x, 1 - h, c) if h == z // 2 else None

    five = five + move(five, from_own(across))
    five = five + sum(move(five, from_own(shift_x(k))) for k in (1, 2, 3))

    offsets = jnp.clip(a_cols - col * 20, 0, 19)
    both = jnp.stack([offsets, move(offsets, flip_h)])
    spread = jnp.stack([both] + [move(both, shift_x(k)) for k in (1, 2, 3)])
    k4 = jnp.arange(4, dtype=jnp.int32)[:, None]
    f2 = jnp.arange(2, dtype=jnp.int32)[None, :]
    ranges = ((x - k4) % 4) * 2 + (h + f2) % 2
    idx = ((ranges[:, :, None, None] * 20 + spread) * BR).reshape(800)

    mine, other = apply_panel(idx, place, p_pieces, a_pieces, five)
    near = mine + move(other, flip_c)
    far = other + move(mine, flip_c)
    low = jnp.where(c == 0, near, far)
    high = jnp.where(c == 0, far, near)
    prolonged = jnp.concatenate([low, high], axis=1).astype(jnp.bfloat16)

    t_own = p_flat.T
    t_pieces = ring(t_own, shift_x) + ring(move(t_own, flip_h), shift_x)
    blocks = project(place, t_pieces, prolonged)
    summed = blocks[0]
    for m in (1, 2, 3):
        summed = summed + move(blocks[m], shift_y(m))
    parts = summed.reshape(2, 128, 2, 128)
    total = None
    for s in range(4):
        k1 = (z // 2 + s // 2) % 2
        l0 = (z + s) % 2
        part = lax.dynamic_slice(parts, (k1, 0, l0, 0), (1, 128, 1, 128)).reshape(128, 128)

        def target(y, z, x, h, c, s=s):
            return (y, ((z // 2 + s // 2) % 2) * 2 + c, x, h, (z + s) % 2)

        got = move(part, target)
        total = got if total is None else total + got
    return total


def solution(mesh):
    placed = (
        P("row", "col", None),
        P("row", "col"),
        P("row", "col"),
        P("row", None, "col"),
        P("row", "col"),
    )
    return jax.shard_map(
        per_device, mesh=mesh, in_specs=placed, out_specs=P("row", "col"), check_vma=False
    )
```

```python
import jax
import jax.numpy as jnp
from jax import lax
from jax.experimental import pallas as pl
from jax.experimental.pallas import tpu as pltpu
from jax.sharding import PartitionSpec as P

BR = 64
AXES = ("row", "col")
STEPS = (0, 1, 3, 2)


def flat(y, z, x, h, c):
    return ((y * 4 + z) * 4 + x) * 4 + h * 2 + c


PLACES = [
    (y, z, x, h, c)
    for y in range(4)
    for z in range(4)
    for x in range(4)
    for h in range(2)
    for c in range(2)
]


def move(array, target):
    pairs = []
    for place in PLACES:
        to = target(*place)
        if to is not None:
            pairs.append((flat(*place), flat(*to)))
    return lax.ppermute(array, AXES, pairs)


def shift_y(k):
    return lambda y, z, x, h, c: ((y + k) % 4, z, x, h, c)


def shift_x(k):
    return lambda y, z, x, h, c: (y, z, (x + k) % 4, h, c)


def flip_h(y, z, x, h, c):
    return (y, z, x, 1 - h, c)


def flip_c(y, z, x, h, c):
    return (y, z, x, h, 1 - c)


def swap_zc(y, z, x, h, c):
    return (y, (z // 2) * 2 + c, x, h, z % 2)


def cross_zc(y, z, x, h, c):
    return (y, (z // 2) * 2 + c, x, 1 - h, z % 2)


def flip_z0(y, z, x, h, c):
    return (y, z ^ 1, x, h, c) if c != z % 2 else None


def after(arrays, *others):
    return lax.optimization_barrier(tuple(arrays) + others)[: len(arrays)]


def scatter_z(s):
    return lambda y, z, x, h, c: (y, (z // 2 ^ s // 2) * 2 + c, x, h, z % 2 ^ s % 2)


def flip_z1(y, z, x, h, c):
    return (y, z ^ 2, x, h, c)


def apply_kernel(place, *refs):
    p_refs = refs[:8]
    a_refs = refs[8:16]
    out = refs[16]
    panel, left, last, ends, numbers, offsets, sems = refs[17:]
    y, z, x, h, c = (place[i] for i in range(5))
    copies = []

    def start(src, dst):
        copy = pltpu.make_async_copy(src, dst, sems.at[len(copies)])
        copy.start()
        copies.append(copy)

    for f in range(2):
        for i in range(4):
            start(a_refs[4 * f + i].at[pl.ds(1280, 16)], ends.at[2 * i + f])
    for i, k in enumerate(STEPS):
        jx = lax.rem(y + 4 - k, 4)
        for s in range(4):
            j1, l0 = lax.rem(z // 2 + s % 2, 2), lax.rem(c + s // 2, 2)
            src = p_refs[4 * (s // 2) + i].at[pl.ds((s % 2) * 1280, 1280)]
            start(src, panel.at[l0, pl.ds(pl.multiple_of((jx * 2 + j1) * 1280, 1280), 1280)])
        start(a_refs[i].at[pl.ds(1296, 320)], last.at[i])
        for f in range(2):
            start(a_refs[4 * f + i].at[pl.ds(0, 1280)], left.at[2 * i + f])

    for copy in copies[:8]:
        copy.wait()
    for slot in range(8):
        numbers[pl.ds(slot, 1), :] = ends[slot][:1, :128].astype(jnp.float32).astype(jnp.int32)
    scalars = pltpu.make_async_copy(numbers, offsets, sems.at[len(copies)])
    scalars.start()
    for copy in copies[8:] + [scalars]:
        copy.wait()

    step = lax.rem(x + 4 - y, 4)
    step = jnp.where(step > 1, 5 - step, step)
    own = step * 2 + lax.rem(h + z // 2, 2)
    bases = []
    for slot in range(8):
        jx = lax.rem(x + 4 - STEPS[slot // 2], 4)
        bases.append((jx * 2 + lax.rem(h + slot % 2, 2)) * 1280)
    own_base = (y * 2 + z // 2) * 1280

    def block(base, slot, at):
        rows = pl.ds(pl.multiple_of(base + offsets[slot, at] * BR, BR), BR)
        return jnp.concatenate([panel[0, rows, :], panel[1, rows, :]], axis=1)

    @pl.loop(0, 20)
    def _(t):
        rows = pl.ds(pl.multiple_of(t * BR, BR), BR)
        fifth = block(own_base, own, t * 5 + 4)
        nothing = jnp.zeros_like(fifth)
        right = jnp.concatenate([jnp.where(t // 5 == q, fifth, nothing) for q in range(4)], axis=0)
        total = jnp.dot(
            last[step, pl.ds(pl.multiple_of(lax.rem(t, 5) * BR, BR), BR), :],
            right,
            preferred_element_type=jnp.float32,
        )
        for slot in range(8):
            blocks = [block(bases[slot], slot, t * 5 + s) for s in range(4)]
            right = jnp.concatenate(blocks, axis=0)
            total += jnp.dot(left[slot, rows, :], right, preferred_element_type=jnp.float32)
        out[rows, :] = total


def apply_panel(place, p_pieces, a_pieces):
    anywhere = pl.BlockSpec(memory_space=pl.ANY)
    return pl.pallas_call(
        apply_kernel,
        out_shape=jax.ShapeDtypeStruct((1280, 256), jnp.float32),
        grid_spec=pltpu.PrefetchScalarGridSpec(
            num_scalar_prefetch=1,
            grid=(),
            in_specs=[anywhere] * 16,
            out_specs=pl.BlockSpec(memory_space=pltpu.VMEM),
            scratch_shapes=[
                pltpu.VMEM((2, 8 * 1280, 128), jnp.bfloat16),
                pltpu.VMEM((8, 1280, 256), jnp.bfloat16),
                pltpu.VMEM((4, 320, 256), jnp.bfloat16),
                pltpu.VMEM((8, 16, 256), jnp.bfloat16),
                pltpu.VMEM((8, 128), jnp.int32),
                pltpu.SMEM((8, 128), jnp.int32),
                pltpu.SemaphoreType.DMA((37,)),
            ],
        ),
        compiler_params=pltpu.CompilerParams(vmem_limit_bytes=56 * 2**20),
        cost_estimate=pl.CostEstimate(
            flops=2 * 1280 * 2048 * 256, bytes_accessed=12 * 2**20, transcendentals=0
        ),
        name="apply_panel",
    )(place, *p_pieces, *a_pieces)


def project_kernel(place, *refs):
    t_refs = refs[:8]
    prol = refs[8]
    outs = refs[9:13]
    left, sems = refs[13:]
    y, x, h = place[0], place[2], place[3]
    copies = []
    for i, k in enumerate(STEPS):
        m = lax.rem(x + 8 - k - y, 4)
        for f in range(2):
            src, dst = t_refs[4 * f + i], left.at[m, lax.rem(h + f, 2)]
            copy = pltpu.make_async_copy(src, dst, sems.at[2 * i + f])
            copy.start()
            copies.append(copy)
    for copy in copies:
        copy.wait()
    for m in range(4):
        for k1 in range(2):
            total = jnp.zeros((128, 256), jnp.float32)
            for i in range(5):
                total += jnp.dot(
                    left[m, k1, pl.ds(i * 128, 128), :],
                    prol[pl.ds(i * 256, 256), :],
                    preferred_element_type=jnp.float32,
                )
            outs[m][pl.ds(k1 * 128, 128), :] = total


def project(place, t_pieces, prol):
    anywhere = pl.BlockSpec(memory_space=pl.ANY)
    inside = pl.BlockSpec(memory_space=pltpu.VMEM)
    out = jax.ShapeDtypeStruct((256, 256), jnp.float32)
    return pl.pallas_call(
        project_kernel,
        out_shape=(out,) * 4,
        grid_spec=pltpu.PrefetchScalarGridSpec(
            num_scalar_prefetch=1,
            grid=(),
            in_specs=[anywhere] * 8 + [inside],
            out_specs=(inside,) * 4,
            scratch_shapes=[
                pltpu.VMEM((4, 2, 640, 256), jnp.bfloat16),
                pltpu.SemaphoreType.DMA((8,)),
            ],
        ),
        compiler_params=pltpu.CompilerParams(vmem_limit_bytes=32 * 2**20),
        cost_estimate=pl.CostEstimate(
            flops=2 * 1280 * 1024 * 256, bytes_accessed=4 * 2**20, transcendentals=0
        ),
        name="project",
    )(place, *t_pieces, prol)


def per_device(a_vals, a_cols, a_count, p_vals, p_mask):
    row, col = lax.axis_index("row"), lax.axis_index("col")
    y, z = row // 4, row % 4
    x, h, c = col // 4, (col // 2) % 2, col % 2
    place = jnp.stack([y, z, x, h, c]).astype(jnp.int32)

    p_live = p_vals * p_mask[:, :, None].astype(jnp.bfloat16)
    p_flat = p_live.reshape(1280, 128)
    p_own = jnp.concatenate([p_flat, move(p_flat, flip_z1)])
    p_twin = move(p_own, flip_c)

    live = jnp.arange(5, dtype=jnp.int32)[None, :] < a_count
    masked = jnp.where(live[:, :, None], a_vals, jnp.zeros_like(a_vals))
    slots = masked.reshape(20, 5, BR, BR)
    four = slots[:, :4].transpose(0, 2, 1, 3).reshape(1280, 256)
    offsets = jnp.clip(a_cols - col * 20, 0, 19).astype(jnp.bfloat16).reshape(1, 100)
    four = jnp.concatenate([four, jnp.pad(offsets, ((0, 15), (0, 156)))])
    swapped = move(four, swap_zc)

    def across(y, z, x, h, c):
        return (y, z, x, 1 - h, c) if h == z // 2 and x == y and c == z % 2 else None

    five = slots[:, 4].reshape(4, 320, BR)
    five = jnp.concatenate([five[q] for q in range(4)], axis=1)
    five = five + move(five, across)

    p_own, p_twin, swapped, four, five = after((p_own, p_twin, swapped, four, five))
    near = jnp.concatenate([swapped, five])
    far = move(four, cross_zc)
    a_near = [near] + [move(near, shift_x(k)) for k in (1, 3, 2)]
    p_mine = [p_own, move(p_own, shift_y(1))]
    far, p_own = after((far, p_own), *p_mine, *a_near)
    a_far = [far] + [move(far, shift_x(k)) for k in (1, 3, 2)]
    p_mine += [move(p_own, shift_y(k)) for k in (3, 2)]
    p_other = [p_twin] + [move(piece, flip_c) for piece in p_mine[1:]]

    t_own = p_flat.reshape(5, 256, 128).transpose(0, 2, 1).reshape(640, 256)
    (t_own,) = after((t_own,), *a_far, *p_other)
    t_far = move(t_own, flip_h)
    t_near = [t_own] + [move(t_own, shift_x(k)) for k in (1, 3, 2)]
    product = apply_panel(place, p_mine + p_other, a_near + a_far)
    product, t_far = after((product, t_far), *t_near)
    t_far = [t_far] + [move(t_far, shift_x(k)) for k in (1, 3, 2)]
    prolonged = (product + move(product, flip_z0)).astype(jnp.bfloat16)
    (prolonged,) = after((prolonged,), *t_near, *t_far)
    prolonged = jnp.where(c == z % 2, prolonged, move(prolonged, flip_c))

    blocks = project(place, t_near + t_far, prolonged)
    summed = blocks[0]
    for m in (1, 2, 3):
        summed = summed + move(blocks[m], shift_y(m))
    parts = summed.reshape(2, 128, 2, 128)
    total = None
    for s in range(4):
        k1 = (z // 2 + s // 2) % 2
        l0 = (z + s) % 2
        part = lax.dynamic_slice(parts, (k1, 0, l0, 0), (1, 128, 1, 128)).reshape(128, 128)
        got = move(part, scatter_z(s))
        total = got if total is None else total + got
    return total


def solution(mesh):
    placed = (
        P("row", "col", None),
        P("row", "col"),
        P("row", "col"),
        P("row", None, "col"),
        P("row", "col"),
    )
    return jax.shard_map(
        per_device, mesh=mesh, in_specs=placed, out_specs=P("row", "col"), check_vma=False
    )
```

```python
import jax
import jax.numpy as jnp
from jax import lax
from jax.experimental import pallas as pl
from jax.experimental.pallas import tpu as pltpu
from jax.sharding import PartitionSpec as P

BR = 64
AXES = ("row", "col")
STEPS = (0, 1, 3, 2)


def flat(y, z, x, h, c):
    return ((y * 4 + z) * 4 + x) * 4 + h * 2 + c


PLACES = [
    (y, z, x, h, c)
    for y in range(4)
    for z in range(4)
    for x in range(4)
    for h in range(2)
    for c in range(2)
]


def move(array, target):
    pairs = []
    for place in PLACES:
        to = target(*place)
        if to is not None:
            pairs.append((flat(*place), flat(*to)))
    return lax.ppermute(array, AXES, pairs)


def shift_y(k):
    return lambda y, z, x, h, c: ((y + k) % 4, z, x, h, c)


def shift_x(k):
    return lambda y, z, x, h, c: (y, z, (x + k) % 4, h, c)


def flip_h(y, z, x, h, c):
    return (y, z, x, 1 - h, c)


def flip_c(y, z, x, h, c):
    return (y, z, x, h, 1 - c)


def swap_zc(y, z, x, h, c):
    return (y, (z // 2) * 2 + c, x, h, z % 2)


def cross_zc(y, z, x, h, c):
    return (y, (z // 2) * 2 + c, x, 1 - h, z % 2)


def flip_z0(y, z, x, h, c):
    return (y, z ^ 1, x, h, c) if c != z % 2 else None


def after(arrays, *others):
    return lax.optimization_barrier(tuple(arrays) + others)[: len(arrays)]


def scatter_z(s):
    return lambda y, z, x, h, c: (y, (z // 2 ^ s // 2) * 2 + c, x, h, z % 2 ^ s % 2)


def flip_z1(y, z, x, h, c):
    return (y, z ^ 2, x, h, c)


def pack_kernel(count, diagonal, blocks, cols, four, five):
    nothing = jnp.zeros((BR, BR), jnp.bfloat16)

    def live(t, s):
        return jnp.where(s < count[t], blocks[t, s], nothing)

    for t in range(20):
        rows = pl.ds(t * BR, BR)
        four[rows, :] = jnp.concatenate([live(t, s) for s in range(4)], axis=1)
    for t in range(5):
        quarters = [live(q * 5 + t, 4) for q in range(4)]
        five[pl.ds(t * BR, BR), :] = jnp.concatenate(quarters, axis=1)
    ends = jnp.clip(cols[...], 0, 19).astype(jnp.float32)
    ends = jnp.concatenate([ends, jnp.zeros((20, 123), jnp.float32)], axis=1)
    ends = jnp.concatenate([ends, jnp.zeros((12, 128), jnp.float32)], axis=0)
    four[pl.ds(1280, 32), :128] = ends.astype(jnp.bfloat16)
    four[pl.ds(1280, 32), 128:] = jnp.zeros((32, 128), jnp.bfloat16)
    own = diagonal[0] == 1
    five[pl.ds(320, 32), :128] = jnp.where(own, ends, 0.0).astype(jnp.bfloat16)
    five[pl.ds(320, 32), 128:] = jnp.zeros((32, 128), jnp.bfloat16)


def pack(count, diagonal, blocks, cols):
    inside = pl.BlockSpec(memory_space=pltpu.VMEM)
    return pl.pallas_call(
        pack_kernel,
        out_shape=(
            jax.ShapeDtypeStruct((1312, 256), jnp.bfloat16),
            jax.ShapeDtypeStruct((352, 256), jnp.bfloat16),
        ),
        grid_spec=pltpu.PrefetchScalarGridSpec(
            num_scalar_prefetch=2,
            grid=(),
            in_specs=[inside, inside],
            out_specs=(inside, inside),
        ),
        cost_estimate=pl.CostEstimate(flops=0, bytes_accessed=3 * 2**20, transcendentals=0),
        name="pack",
    )(count, diagonal, blocks, cols)


def apply_kernel(place, *refs):
    p_refs = refs[:8]
    a_refs = refs[8:16]
    out = refs[16]
    panel, left, ends, numbers, offsets, sems = refs[17:]
    y, z, x, h, c = (place[i] for i in range(5))
    copies = []

    def start(src, dst):
        copy = pltpu.make_async_copy(src, dst, sems.at[len(copies)])
        copy.start()
        copies.append(copy)

    for f in range(2):
        for i in range(4):
            start(a_refs[4 * f + i].at[pl.ds(1280, 32)], ends.at[2 * i + f])
    for i, k in enumerate(STEPS):
        jx = lax.rem(y + 4 - k, 4)
        for s in range(4):
            j1, l0 = lax.rem(z // 2 + s % 2, 2), lax.rem(c + s // 2, 2)
            src = p_refs[4 * (s // 2) + i].at[pl.ds((s % 2) * 1280, 1280)]
            start(src, panel.at[l0, pl.ds(pl.multiple_of((jx * 2 + j1) * 1280, 1280), 1280)])
        for f in range(2):
            start(a_refs[4 * f + i].at[pl.ds(0, 1280)], left.at[2 * i + f])

    for copy in copies[:8]:
        copy.wait()
    for slot in range(8):
        numbers[slot] = ends[slot][:24, :128].astype(jnp.float32).astype(jnp.int32)
    scalars = pltpu.make_async_copy(numbers, offsets, sems.at[len(copies)])
    scalars.start()
    for copy in copies[8:] + [scalars]:
        copy.wait()

    bases = []
    for slot in range(8):
        jx = lax.rem(x + 4 - STEPS[slot // 2], 4)
        bases.append((jx * 2 + lax.rem(h + slot % 2, 2)) * 1280)

    def block(base, slot, at):
        rows = pl.ds(pl.multiple_of(base + offsets[slot, at[0], at[1]] * BR, BR), BR)
        return jnp.concatenate([panel[0, rows, :], panel[1, rows, :]], axis=1)

    @pl.loop(0, 20)
    def _(t):
        rows = pl.ds(pl.multiple_of(t * BR, BR), BR)
        total = jnp.zeros((BR, 256), jnp.float32)
        for slot in range(8):
            blocks = [block(bases[slot], slot, (t, s)) for s in range(4)]
            right = jnp.concatenate(blocks, axis=0)
            total += jnp.dot(left[slot, rows, :], right, preferred_element_type=jnp.float32)
        out[rows, :] = total


def apply_panel(place, p_pieces, a_pieces):
    anywhere = pl.BlockSpec(memory_space=pl.ANY)
    inside = pl.BlockSpec(memory_space=pltpu.VMEM)
    return pl.pallas_call(
        apply_kernel,
        out_shape=jax.ShapeDtypeStruct((1280, 256), jnp.float32),
        grid_spec=pltpu.PrefetchScalarGridSpec(
            num_scalar_prefetch=1,
            grid=(),
            in_specs=[anywhere] * 16,
            out_specs=inside,
            scratch_shapes=[
                pltpu.VMEM((2, 8 * 1280, 128), jnp.bfloat16),
                pltpu.VMEM((8, 1280, 256), jnp.bfloat16),
                pltpu.VMEM((8, 32, 256), jnp.bfloat16),
                pltpu.VMEM((8, 24, 128), jnp.int32),
                pltpu.SMEM((8, 24, 128), jnp.int32),
                pltpu.SemaphoreType.DMA((33,)),
            ],
        ),
        compiler_params=pltpu.CompilerParams(vmem_limit_bytes=56 * 2**20),
        cost_estimate=pl.CostEstimate(
            flops=2 * 1280 * 2048 * 256, bytes_accessed=12 * 2**20, transcendentals=0
        ),
        name="apply_panel",
    )(place, *p_pieces, *a_pieces)


def last_kernel(place, mine, other, five, out, panel, numbers, offsets, sems):
    c = place[4]
    copies = []
    for n, src in enumerate((mine, other)):
        dst = panel.at[lax.rem(c + n, 2)]
        copies.append(pltpu.make_async_copy(src.at[pl.ds(0, 1280)], dst, sems.at[n]))
        copies[n].start()
    numbers[...] = five[pl.ds(320, 32), :128][:24].astype(jnp.float32).astype(jnp.int32)
    scalars = pltpu.make_async_copy(numbers, offsets, sems.at[2])
    scalars.start()
    for copy in copies + [scalars]:
        copy.wait()

    @pl.loop(0, 20)
    def _(t):
        rows = pl.ds(pl.multiple_of(offsets[t, 4] * BR, BR), BR)
        block = jnp.concatenate([panel[0, rows, :], panel[1, rows, :]], axis=1)
        nothing = jnp.zeros_like(block)
        right = jnp.concatenate([jnp.where(t // 5 == q, block, nothing) for q in range(4)], axis=0)
        out[pl.ds(pl.multiple_of(t * BR, BR), BR), :] = jnp.dot(
            five[pl.ds(pl.multiple_of(lax.rem(t, 5) * BR, BR), BR), :],
            right,
            preferred_element_type=jnp.float32,
        )


def apply_last(place, mine, other, five):
    anywhere = pl.BlockSpec(memory_space=pl.ANY)
    inside = pl.BlockSpec(memory_space=pltpu.VMEM)
    return pl.pallas_call(
        last_kernel,
        out_shape=jax.ShapeDtypeStruct((1280, 256), jnp.float32),
        grid_spec=pltpu.PrefetchScalarGridSpec(
            num_scalar_prefetch=1,
            grid=(),
            in_specs=[anywhere, anywhere, inside],
            out_specs=inside,
            scratch_shapes=[
                pltpu.VMEM((2, 1280, 128), jnp.bfloat16),
                pltpu.VMEM((24, 128), jnp.int32),
                pltpu.SMEM((24, 128), jnp.int32),
                pltpu.SemaphoreType.DMA((3,)),
            ],
        ),
        cost_estimate=pl.CostEstimate(
            flops=2 * 1280 * 256 * 256, bytes_accessed=2 * 2**20, transcendentals=0
        ),
        name="apply_last",
    )(place, mine, other, five)


def project_kernel(place, *refs):
    t_refs = refs[:8]
    prol = refs[8]
    outs = refs[9:13]
    left, sems = refs[13:]
    y, x, h = place[0], place[2], place[3]
    copies = []
    for i, k in enumerate(STEPS):
        m = lax.rem(x + 8 - k - y, 4)
        for f in range(2):
            src, dst = t_refs[4 * f + i], left.at[m, lax.rem(h + f, 2)]
            copy = pltpu.make_async_copy(src, dst, sems.at[2 * i + f])
            copy.start()
            copies.append(copy)
    for copy in copies:
        copy.wait()
    for m in range(4):
        for k1 in range(2):
            total = jnp.zeros((128, 256), jnp.float32)
            for i in range(5):
                total += jnp.dot(
                    left[m, k1, pl.ds(i * 128, 128), :],
                    prol[pl.ds(i * 256, 256), :],
                    preferred_element_type=jnp.float32,
                )
            outs[m][pl.ds(k1 * 128, 128), :] = total


def project(place, t_pieces, prol):
    anywhere = pl.BlockSpec(memory_space=pl.ANY)
    inside = pl.BlockSpec(memory_space=pltpu.VMEM)
    out = jax.ShapeDtypeStruct((256, 256), jnp.float32)
    return pl.pallas_call(
        project_kernel,
        out_shape=(out,) * 4,
        grid_spec=pltpu.PrefetchScalarGridSpec(
            num_scalar_prefetch=1,
            grid=(),
            in_specs=[anywhere] * 8 + [inside],
            out_specs=(inside,) * 4,
            scratch_shapes=[
                pltpu.VMEM((4, 2, 640, 256), jnp.bfloat16),
                pltpu.SemaphoreType.DMA((8,)),
            ],
        ),
        compiler_params=pltpu.CompilerParams(vmem_limit_bytes=32 * 2**20),
        cost_estimate=pl.CostEstimate(
            flops=2 * 1280 * 1024 * 256, bytes_accessed=4 * 2**20, transcendentals=0
        ),
        name="project",
    )(place, *t_pieces, prol)


def per_device(a_vals, a_cols, a_count, p_vals, p_mask):
    row, col = lax.axis_index("row"), lax.axis_index("col")
    y, z = row // 4, row % 4
    x, h, c = col // 4, (col // 2) % 2, col % 2
    place = jnp.stack([y, z, x, h, c]).astype(jnp.int32)

    p_live = p_vals * p_mask[:, :, None].astype(jnp.bfloat16)
    p_flat = p_live.reshape(1280, 128)
    p_own = jnp.concatenate([p_flat, move(p_flat, flip_z1)])
    p_twin = move(p_own, flip_c)

    diagonal = (row == col).astype(jnp.int32).reshape(1)
    four, five = pack(a_count.reshape(20), diagonal, a_vals.reshape(20, 5, BR, BR), a_cols - col * 20)
    swapped = move(four, swap_zc)

    def across(y, z, x, h, c):
        return (y, z, x, 1 - h, c) if h == z // 2 and x == y and c == z % 2 else None

    def next_x(y, z, x, h, c):
        return (y, z, (x + 1) % 4, h, c) if x == y and c == z % 2 else None

    def over_x(y, z, x, h, c):
        return (y, z, (x + 2) % 4, h, c) if (x - y) % 4 < 2 and c == z % 2 else None


    p_own, near, four = after((p_own, swapped, four))
    far = move(four, cross_zc)
    a_near = [near] + [move(near, shift_x(k)) for k in (1, 3, 2)]
    p_mine = [p_own, move(p_own, shift_y(1))]
    far, p_own = after((far, p_own), *p_mine, *a_near)
    a_far = [far] + [move(far, shift_x(k)) for k in (1, 3, 2)]
    p_mine += [move(p_own, shift_y(k)) for k in (3, 2)]
    p_other = [p_twin] + [move(piece, flip_c) for piece in p_mine[1:]]

    t_own = p_flat.reshape(5, 256, 128).transpose(0, 2, 1).reshape(640, 256)
    t_own, five = after((t_own, five), *a_far, *p_other)
    t_far = move(t_own, flip_h)
    t_near = [t_own] + [move(t_own, shift_x(k)) for k in (1, 3, 2)]
    five = five + move(five, across)
    product = apply_panel(place, p_mine + p_other, a_near + a_far)
    product, t_far, five = after((product, t_far, five), *t_near)
    t_far = [t_far] + [move(t_far, shift_x(k)) for k in (1, 3, 2)]
    five = five + move(five, next_x)
    five = five + move(five, over_x)
    extra = apply_last(place, p_mine[0], p_other[0], five)
    prolonged = (product + extra + move(product, flip_z0)).astype(jnp.bfloat16)
    (prolonged,) = after((prolonged,), *t_near, *t_far)
    prolonged = jnp.where(c == z % 2, prolonged, move(prolonged, flip_c))

    blocks = project(place, t_near + t_far, prolonged)
    summed = blocks[0]
    for m in (1, 2, 3):
        summed = summed + move(blocks[m], shift_y(m))
    parts = summed.reshape(2, 128, 2, 128)
    total = None
    for s in range(4):
        k1 = (z // 2 + s // 2) % 2
        l0 = (z + s) % 2
        part = lax.dynamic_slice(parts, (k1, 0, l0, 0), (1, 128, 1, 128)).reshape(128, 128)
        got = move(part, scatter_z(s))
        total = got if total is None else total + got
    return total


def solution(mesh):
    placed = (
        P("row", "col", None),
        P("row", "col"),
        P("row", "col"),
        P("row", None, "col"),
        P("row", "col"),
    )
    return jax.shard_map(
        per_device, mesh=mesh, in_specs=placed, out_specs=P("row", "col"), check_vma=False
    )
```

```python
import jax
import jax.numpy as jnp
from jax import lax
from jax.experimental import pallas as pl
from jax.experimental.pallas import tpu as pltpu
from jax.sharding import PartitionSpec as P

BR = 64
AXES = ("row", "col")
STEPS = (0, 1, 3, 2)


def flat(y, z, x, h, c):
    return ((y * 4 + z) * 4 + x) * 4 + h * 2 + c


PLACES = [
    (y, z, x, h, c)
    for y in range(4)
    for z in range(4)
    for x in range(4)
    for h in range(2)
    for c in range(2)
]


def move(array, target):
    pairs = []
    for place in PLACES:
        to = target(*place)
        if to is not None:
            pairs.append((flat(*place), flat(*to)))
    return lax.ppermute(array, AXES, pairs)


def shift_y(k):
    return lambda y, z, x, h, c: ((y + k) % 4, z, x, h, c)


def shift_x(k):
    return lambda y, z, x, h, c: (y, z, (x + k) % 4, h, c)


def flip_h(y, z, x, h, c):
    return (y, z, x, 1 - h, c)


def flip_c(y, z, x, h, c):
    return (y, z, x, h, 1 - c)


def swap_zc(y, z, x, h, c):
    return (y, (z // 2) * 2 + c, x, h, z % 2)


def cross_zc(y, z, x, h, c):
    return (y, (z // 2) * 2 + c, x, 1 - h, z % 2)


def flip_z0(y, z, x, h, c):
    return (y, z ^ 1, x, h, c) if c != z % 2 else None


def after(arrays, *others):
    return lax.optimization_barrier(tuple(arrays) + others)[: len(arrays)]


def scatter_z(s):
    return lambda y, z, x, h, c: (y, (z // 2 ^ s // 2) * 2 + c, x, h, z % 2 ^ s % 2)


def flip_z1(y, z, x, h, c):
    return (y, z ^ 2, x, h, c)


def pack_kernel(count, diagonal, blocks, cols, four, five):
    nothing = jnp.zeros((BR, BR), jnp.bfloat16)

    def live(t, s):
        return jnp.where(s < count[t], blocks[t, s], nothing)

    for t in range(20):
        rows = pl.ds(t * BR, BR)
        four[rows, :] = jnp.concatenate([live(t, s) for s in range(4)], axis=1)
    for t in range(5):
        quarters = [live(q * 5 + t, 4) for q in range(4)]
        five[pl.ds(t * BR, BR), :] = jnp.concatenate(quarters, axis=1)
    ends = jnp.clip(cols[...], 0, 19).astype(jnp.float32)
    ends = jnp.concatenate([ends, jnp.zeros((20, 123), jnp.float32)], axis=1)
    ends = jnp.concatenate([ends, jnp.zeros((12, 128), jnp.float32)], axis=0)
    four[pl.ds(1280, 32), :128] = ends.astype(jnp.bfloat16)
    four[pl.ds(1280, 32), 128:] = jnp.zeros((32, 128), jnp.bfloat16)
    own = diagonal[0] == 1
    five[pl.ds(320, 32), :128] = jnp.where(own, ends, 0.0).astype(jnp.bfloat16)
    five[pl.ds(320, 32), 128:] = jnp.zeros((32, 128), jnp.bfloat16)


def pack(count, diagonal, blocks, cols):
    inside = pl.BlockSpec(memory_space=pltpu.VMEM)
    return pl.pallas_call(
        pack_kernel,
        out_shape=(
            jax.ShapeDtypeStruct((1312, 256), jnp.bfloat16),
            jax.ShapeDtypeStruct((352, 256), jnp.bfloat16),
        ),
        grid_spec=pltpu.PrefetchScalarGridSpec(
            num_scalar_prefetch=2,
            grid=(),
            in_specs=[inside, inside],
            out_specs=(inside, inside),
        ),
        cost_estimate=pl.CostEstimate(flops=0, bytes_accessed=3 * 2**20, transcendentals=0),
        name="pack",
    )(count, diagonal, blocks, cols)


def apply_kernel(place, *refs):
    p_refs = refs[:8]
    a_refs = refs[8:16]
    out = refs[16]
    panel, left, ends, numbers, offsets, sems = refs[17:]
    y, z, x, h, c = (place[i] for i in range(5))
    copies = []

    def start(src, dst):
        copy = pltpu.make_async_copy(src, dst, sems.at[len(copies)])
        copy.start()
        copies.append(copy)

    for f in range(2):
        for i in range(4):
            start(a_refs[4 * f + i].at[pl.ds(1280, 32)], ends.at[2 * i + f])
    for i, k in enumerate(STEPS):
        jx = lax.rem(y + 4 - k, 4)
        for s in range(4):
            j1, l0 = lax.rem(z // 2 + s % 2, 2), lax.rem(c + s // 2, 2)
            src = p_refs[4 * (s // 2) + i].at[pl.ds((s % 2) * 1280, 1280)]
            start(src, panel.at[l0, pl.ds(pl.multiple_of((jx * 2 + j1) * 1280, 1280), 1280)])
        for f in range(2):
            start(a_refs[4 * f + i].at[pl.ds(0, 1280)], left.at[2 * i + f])

    for copy in copies[:8]:
        copy.wait()
    for slot in range(8):
        numbers[slot] = ends[slot][:24, :128].astype(jnp.float32).astype(jnp.int32)
    scalars = pltpu.make_async_copy(numbers, offsets, sems.at[len(copies)])
    scalars.start()
    for copy in copies[8:] + [scalars]:
        copy.wait()

    bases = []
    for slot in range(8):
        jx = lax.rem(x + 4 - STEPS[slot // 2], 4)
        bases.append((jx * 2 + lax.rem(h + slot % 2, 2)) * 1280)

    def block(base, slot, at):
        rows = pl.ds(pl.multiple_of(base + offsets[slot, at[0], at[1]] * BR, BR), BR)
        return jnp.concatenate([panel[0, rows, :], panel[1, rows, :]], axis=1)

    @pl.loop(0, 20)
    def _(t):
        rows = pl.ds(pl.multiple_of(t * BR, BR), BR)
        total = jnp.zeros((BR, 256), jnp.float32)
        for slot in range(8):
            blocks = [block(bases[slot], slot, (t, s)) for s in range(4)]
            right = jnp.concatenate(blocks, axis=0)
            total += jnp.dot(left[slot, rows, :], right, preferred_element_type=jnp.float32)
        out[rows, :] = total


def apply_panel(place, p_pieces, a_pieces):
    anywhere = pl.BlockSpec(memory_space=pl.ANY)
    inside = pl.BlockSpec(memory_space=pltpu.VMEM)
    return pl.pallas_call(
        apply_kernel,
        out_shape=jax.ShapeDtypeStruct((1280, 256), jnp.float32),
        grid_spec=pltpu.PrefetchScalarGridSpec(
            num_scalar_prefetch=1,
            grid=(),
            in_specs=[anywhere] * 16,
            out_specs=inside,
            scratch_shapes=[
                pltpu.VMEM((2, 8 * 1280, 128), jnp.bfloat16),
                pltpu.VMEM((8, 1280, 256), jnp.bfloat16),
                pltpu.VMEM((8, 32, 256), jnp.bfloat16),
                pltpu.VMEM((8, 24, 128), jnp.int32),
                pltpu.SMEM((8, 24, 128), jnp.int32),
                pltpu.SemaphoreType.DMA((33,)),
            ],
        ),
        compiler_params=pltpu.CompilerParams(vmem_limit_bytes=56 * 2**20),
        cost_estimate=pl.CostEstimate(
            flops=2 * 1280 * 2048 * 256, bytes_accessed=12 * 2**20, transcendentals=0
        ),
        name="apply_panel",
    )(place, *p_pieces, *a_pieces)


def last_kernel(place, mine, other, five, before, out, panel, numbers, offsets, sems):
    c = place[4]
    copies = []
    for n, src in enumerate((mine, other)):
        dst = panel.at[lax.rem(c + n, 2)]
        copies.append(pltpu.make_async_copy(src.at[pl.ds(0, 1280)], dst, sems.at[n]))
        copies[n].start()
    numbers[...] = five[pl.ds(320, 32), :128][:24].astype(jnp.float32).astype(jnp.int32)
    scalars = pltpu.make_async_copy(numbers, offsets, sems.at[2])
    scalars.start()
    for copy in copies + [scalars]:
        copy.wait()

    for t in range(20):
        rows = pl.ds(pl.multiple_of(offsets[t, 4] * BR, BR), BR)
        block = jnp.concatenate([panel[0, rows, :], panel[1, rows, :]], axis=1)
        extra = jnp.dot(
            five[pl.ds(t % 5 * BR, BR), pl.ds(t // 5 * BR, BR)],
            block,
            preferred_element_type=jnp.float32,
        )
        out[pl.ds(t * BR, BR), :] = before[pl.ds(t * BR, BR), :] + extra


def apply_last(place, mine, other, five, before):
    anywhere = pl.BlockSpec(memory_space=pl.ANY)
    inside = pl.BlockSpec(memory_space=pltpu.VMEM)
    return pl.pallas_call(
        last_kernel,
        out_shape=jax.ShapeDtypeStruct((1280, 256), jnp.float32),
        grid_spec=pltpu.PrefetchScalarGridSpec(
            num_scalar_prefetch=1,
            grid=(),
            in_specs=[anywhere, anywhere, inside, inside],
            out_specs=inside,
            scratch_shapes=[
                pltpu.VMEM((2, 1280, 128), jnp.bfloat16),
                pltpu.VMEM((24, 128), jnp.int32),
                pltpu.SMEM((24, 128), jnp.int32),
                pltpu.SemaphoreType.DMA((3,)),
            ],
        ),
        cost_estimate=pl.CostEstimate(
            flops=2 * 1280 * 256 * 256, bytes_accessed=2 * 2**20, transcendentals=0
        ),
        name="apply_last",
    )(place, mine, other, five, before)


def project_kernel(place, *refs):
    t_refs = refs[:8]
    mine, twin = refs[8:10]
    outs = refs[10:14]
    left, prol, sems = refs[14:]
    y, z, x, h, c = (place[i] for i in range(5))
    copies = []
    for i, k in enumerate(STEPS):
        m = lax.rem(x + 8 - k - y, 4)
        for f in range(2):
            src, dst = t_refs[4 * f + i], left.at[m, lax.rem(h + f, 2)]
            copy = pltpu.make_async_copy(src, dst, sems.at[2 * i + f])
            copy.start()
            copies.append(copy)
    prol[...] = jnp.where(c == lax.rem(z, 2), mine[...], twin[...])
    for copy in copies:
        copy.wait()
    for m in range(4):
        for k1 in range(2):
            total = jnp.zeros((128, 256), jnp.float32)
            for i in range(5):
                total += jnp.dot(
                    left[m, k1, pl.ds(i * 128, 128), :],
                    prol[pl.ds(i * 256, 256), :],
                    preferred_element_type=jnp.float32,
                )
            outs[m][pl.ds(k1 * 128, 128), :] = total


def project(place, t_pieces, mine, twin):
    anywhere = pl.BlockSpec(memory_space=pl.ANY)
    inside = pl.BlockSpec(memory_space=pltpu.VMEM)
    out = jax.ShapeDtypeStruct((256, 256), jnp.float32)
    return pl.pallas_call(
        project_kernel,
        out_shape=(out,) * 4,
        grid_spec=pltpu.PrefetchScalarGridSpec(
            num_scalar_prefetch=1,
            grid=(),
            in_specs=[anywhere] * 8 + [inside] * 2,
            out_specs=(inside,) * 4,
            scratch_shapes=[
                pltpu.VMEM((4, 2, 640, 256), jnp.bfloat16),
                pltpu.VMEM((1280, 256), jnp.bfloat16),
                pltpu.SemaphoreType.DMA((8,)),
            ],
        ),
        compiler_params=pltpu.CompilerParams(vmem_limit_bytes=32 * 2**20),
        cost_estimate=pl.CostEstimate(
            flops=2 * 1280 * 1024 * 256, bytes_accessed=4 * 2**20, transcendentals=0
        ),
        name="project",
    )(place, *t_pieces, mine, twin)


def per_device(a_vals, a_cols, a_count, p_vals, p_mask):
    row, col = lax.axis_index("row"), lax.axis_index("col")
    y, z = row // 4, row % 4
    x, h, c = col // 4, (col // 2) % 2, col % 2
    place = jnp.stack([y, z, x, h, c]).astype(jnp.int32)

    p_live = p_vals * p_mask[:, :, None].astype(jnp.bfloat16)
    p_flat = p_live.reshape(1280, 128)
    p_own = jnp.concatenate([p_flat, move(p_flat, flip_z1)])
    p_twin = move(p_own, flip_c)

    diagonal = (row == col).astype(jnp.int32).reshape(1)
    four, five = pack(a_count.reshape(20), diagonal, a_vals.reshape(20, 5, BR, BR), a_cols - col * 20)
    swapped = move(four, swap_zc)

    def across(y, z, x, h, c):
        return (y, z, x, 1 - h, c) if h == z // 2 and x == y and c == z % 2 else None

    def next_x(y, z, x, h, c):
        return (y, z, (x + 1) % 4, h, c) if x == y and c == z % 2 else None

    def over_x(y, z, x, h, c):
        return (y, z, (x + 2) % 4, h, c) if (x - y) % 4 < 2 and c == z % 2 else None


    p_own, near, four = after((p_own, swapped, four))
    far = move(four, cross_zc)
    a_near = [near] + [move(near, shift_x(k)) for k in (1, 3, 2)]
    p_mine = [p_own, move(p_own, shift_y(1))]
    far, p_own = after((far, p_own), *p_mine, *a_near)
    a_far = [far] + [move(far, shift_x(k)) for k in (1, 3, 2)]
    p_mine += [move(p_own, shift_y(k)) for k in (3, 2)]
    p_other = [p_twin] + [move(piece, flip_c) for piece in p_mine[1:]]

    t_own = p_flat.reshape(5, 256, 128).transpose(0, 2, 1).reshape(640, 256)
    t_own, five = after((t_own, five), *a_far, *p_other)
    t_far = move(t_own, flip_h)
    t_near = [t_own] + [move(t_own, shift_x(k)) for k in (1, 3, 2)]
    five = five + move(five, across)
    product = apply_panel(place, p_mine + p_other, a_near + a_far)
    product, t_far, five = after((product, t_far, five), *t_near)
    t_far = [t_far] + [move(t_far, shift_x(k)) for k in (1, 3, 2)]
    five = five + move(five, next_x)
    five = five + move(five, over_x)
    total = apply_last(place, p_mine[0], p_other[0], five, product)
    prolonged = (total + move(product, flip_z0)).astype(jnp.bfloat16)
    (prolonged,) = after((prolonged,), *t_near, *t_far)
    twin = move(prolonged, flip_c)

    blocks = project(place, t_near + t_far, prolonged, twin)
    summed = blocks[0]
    for m in (1, 2, 3):
        summed = summed + move(blocks[m], shift_y(m))
    parts = summed.reshape(2, 128, 2, 128)
    total = None
    for s in range(4):
        k1 = (z // 2 + s // 2) % 2
        l0 = (z + s) % 2
        part = lax.dynamic_slice(parts, (k1, 0, l0, 0), (1, 128, 1, 128)).reshape(128, 128)
        got = move(part, scatter_z(s))
        total = got if total is None else total + got
    return total


def solution(mesh):
    placed = (
        P("row", "col", None),
        P("row", "col"),
        P("row", "col"),
        P("row", None, "col"),
        P("row", "col"),
    )
    return jax.shard_map(
        per_device, mesh=mesh, in_specs=placed, out_specs=P("row", "col"), check_vma=False
    )
```

```python
import jax
import jax.numpy as jnp
from jax import lax
from jax.experimental import pallas as pl
from jax.experimental.pallas import tpu as pltpu
from jax.sharding import PartitionSpec as P

BR = 64
AXES = ("row", "col")
STEPS = (0, 1, 3, 2)


def flat(y, z, x, h, c):
    return ((y * 4 + z) * 4 + x) * 4 + h * 2 + c


PLACES = [
    (y, z, x, h, c)
    for y in range(4)
    for z in range(4)
    for x in range(4)
    for h in range(2)
    for c in range(2)
]


def move(array, target):
    pairs = []
    for place in PLACES:
        to = target(*place)
        if to is not None:
            pairs.append((flat(*place), flat(*to)))
    return lax.ppermute(array, AXES, pairs)


def shift_y(k):
    return lambda y, z, x, h, c: ((y + k) % 4, z, x, h, c)


def shift_x(k):
    return lambda y, z, x, h, c: (y, z, (x + k) % 4, h, c)


def flip_h(y, z, x, h, c):
    return (y, z, x, 1 - h, c)


def flip_c(y, z, x, h, c):
    return (y, z, x, h, 1 - c)


def swap_zc(y, z, x, h, c):
    return (y, (z // 2) * 2 + c, x, h, z % 2)


def cross_zc(y, z, x, h, c):
    return (y, (z // 2) * 2 + c, x, 1 - h, z % 2)


def flip_z0(y, z, x, h, c):
    return (y, z ^ 1, x, h, c) if c != z % 2 else None


def after(arrays, *others):
    return lax.optimization_barrier(tuple(arrays) + others)[: len(arrays)]


def scatter_z(s):
    return lambda y, z, x, h, c: (y, (z // 2 ^ s // 2) * 2 + c, x, h, z % 2 ^ s % 2)


def flip_z1(y, z, x, h, c):
    return (y, z ^ 2, x, h, c)


def pack_kernel(count, diagonal, blocks, cols, four, five):
    nothing = jnp.zeros((BR, BR), jnp.bfloat16)

    def live(t, s):
        return jnp.where(s < count[t], blocks[t, s], nothing)

    for t in range(20):
        rows = pl.ds(t * BR, BR)
        four[rows, :] = jnp.concatenate([live(t, s) for s in range(4)], axis=1)
    for t in range(5):
        quarters = [live(q * 5 + t, 4) for q in range(4)]
        five[pl.ds(t * BR, BR), :] = jnp.concatenate(quarters, axis=1)
    ends = jnp.clip(cols[...], 0, 19).astype(jnp.float32)
    ends = jnp.concatenate([ends, jnp.zeros((20, 123), jnp.float32)], axis=1)
    ends = jnp.concatenate([ends, jnp.zeros((12, 128), jnp.float32)], axis=0)
    four[pl.ds(1280, 32), :128] = ends.astype(jnp.bfloat16)
    four[pl.ds(1280, 32), 128:] = jnp.zeros((32, 128), jnp.bfloat16)
    own = diagonal[0] == 1
    five[pl.ds(320, 32), :128] = jnp.where(own, ends, 0.0).astype(jnp.bfloat16)
    five[pl.ds(320, 32), 128:] = jnp.zeros((32, 128), jnp.bfloat16)


def pack(count, diagonal, blocks, cols):
    inside = pl.BlockSpec(memory_space=pltpu.VMEM)
    return pl.pallas_call(
        pack_kernel,
        out_shape=(
            jax.ShapeDtypeStruct((1312, 256), jnp.bfloat16),
            jax.ShapeDtypeStruct((352, 256), jnp.bfloat16),
        ),
        grid_spec=pltpu.PrefetchScalarGridSpec(
            num_scalar_prefetch=2,
            grid=(),
            in_specs=[inside, inside],
            out_specs=(inside, inside),
        ),
        cost_estimate=pl.CostEstimate(flops=0, bytes_accessed=3 * 2**20, transcendentals=0),
        name="pack",
    )(count, diagonal, blocks, cols)


def apply_kernel(place, *refs):
    p_refs = refs[:8]
    a_refs = refs[8:16]
    out = refs[16]
    panel, left, ends, numbers, offsets, sems = refs[17:]
    y, z, x, h, c = (place[i] for i in range(5))
    copies = []

    def start(src, dst):
        copy = pltpu.make_async_copy(src, dst, sems.at[len(copies)])
        copy.start()
        copies.append(copy)

    for f in range(2):
        for i in range(4):
            start(a_refs[4 * f + i].at[pl.ds(1280, 32)], ends.at[2 * i + f])
    for i, k in enumerate(STEPS):
        jx = lax.rem(y + 4 - k, 4)
        for s in range(4):
            j1, l0 = lax.rem(z // 2 + s % 2, 2), lax.rem(c + s // 2, 2)
            src = p_refs[4 * (s // 2) + i].at[pl.ds((s % 2) * 1280, 1280)]
            start(src, panel.at[l0, pl.ds(pl.multiple_of((jx * 2 + j1) * 1280, 1280), 1280)])
        for f in range(2):
            start(a_refs[4 * f + i].at[pl.ds(0, 1280)], left.at[2 * i + f])

    for copy in copies[:8]:
        copy.wait()
    for slot in range(8):
        numbers[slot] = ends[slot][:, :128].astype(jnp.float32)[:24].astype(jnp.int32)
    scalars = pltpu.make_async_copy(numbers, offsets, sems.at[len(copies)])
    scalars.start()
    for copy in copies[8:] + [scalars]:
        copy.wait()

    bases = []
    for slot in range(8):
        jx = lax.rem(x + 4 - STEPS[slot // 2], 4)
        bases.append((jx * 2 + lax.rem(h + slot % 2, 2)) * 1280)

    def block(base, slot, at):
        rows = pl.ds(pl.multiple_of(base + offsets[slot, at[0], at[1]] * BR, BR), BR)
        return jnp.concatenate([panel[0, rows, :], panel[1, rows, :]], axis=1)

    @pl.loop(0, 20)
    def _(t):
        rows = pl.ds(pl.multiple_of(t * BR, BR), BR)
        total = jnp.zeros((BR, 256), jnp.float32)
        for slot in range(8):
            blocks = [block(bases[slot], slot, (t, s)) for s in range(4)]
            right = jnp.concatenate(blocks, axis=0)
            total += jnp.dot(left[slot, rows, :], right, preferred_element_type=jnp.float32)
        out[rows, :] = total


def apply_panel(place, p_pieces, a_pieces):
    anywhere = pl.BlockSpec(memory_space=pl.ANY)
    inside = pl.BlockSpec(memory_space=pltpu.VMEM)
    return pl.pallas_call(
        apply_kernel,
        out_shape=jax.ShapeDtypeStruct((1280, 256), jnp.float32),
        grid_spec=pltpu.PrefetchScalarGridSpec(
            num_scalar_prefetch=1,
            grid=(),
            in_specs=[anywhere] * 16,
            out_specs=inside,
            scratch_shapes=[
                pltpu.VMEM((2, 8 * 1280, 128), jnp.bfloat16),
                pltpu.VMEM((8, 1280, 256), jnp.bfloat16),
                pltpu.VMEM((8, 32, 256), jnp.bfloat16),
                pltpu.VMEM((8, 24, 128), jnp.int32),
                pltpu.SMEM((8, 24, 128), jnp.int32),
                pltpu.SemaphoreType.DMA((33,)),
            ],
        ),
        compiler_params=pltpu.CompilerParams(vmem_limit_bytes=56 * 2**20),
        cost_estimate=pl.CostEstimate(
            flops=2 * 1280 * 2048 * 256, bytes_accessed=12 * 2**20, transcendentals=0
        ),
        name="apply_panel",
    )(place, *p_pieces, *a_pieces)


def last_kernel(place, mine, other, five, before, out, panel, numbers, offsets, sems):
    c = place[4]
    copies = []
    for n, src in enumerate((mine, other)):
        dst = panel.at[lax.rem(c + n, 2)]
        copies.append(pltpu.make_async_copy(src.at[pl.ds(0, 1280)], dst, sems.at[n]))
        copies[n].start()
    numbers[...] = five[pl.ds(320, 32), :128].astype(jnp.float32)[:24].astype(jnp.int32)
    scalars = pltpu.make_async_copy(numbers, offsets, sems.at[2])
    scalars.start()
    for copy in copies + [scalars]:
        copy.wait()

    for t in range(20):
        rows = pl.ds(pl.multiple_of(offsets[t, 4] * BR, BR), BR)
        block = jnp.concatenate([panel[0, rows, :], panel[1, rows, :]], axis=1)
        extra = jnp.dot(
            five[pl.ds(t % 5 * BR, BR), pl.ds(t // 5 * BR, BR)],
            block,
            preferred_element_type=jnp.float32,
        )
        out[pl.ds(t * BR, BR), :] = before[pl.ds(t * BR, BR), :] + extra


def apply_last(place, mine, other, five, before):
    anywhere = pl.BlockSpec(memory_space=pl.ANY)
    inside = pl.BlockSpec(memory_space=pltpu.VMEM)
    return pl.pallas_call(
        last_kernel,
        out_shape=jax.ShapeDtypeStruct((1280, 256), jnp.float32),
        grid_spec=pltpu.PrefetchScalarGridSpec(
            num_scalar_prefetch=1,
            grid=(),
            in_specs=[anywhere, anywhere, inside, inside],
            out_specs=inside,
            scratch_shapes=[
                pltpu.VMEM((2, 1280, 128), jnp.bfloat16),
                pltpu.VMEM((24, 128), jnp.int32),
                pltpu.SMEM((24, 128), jnp.int32),
                pltpu.SemaphoreType.DMA((3,)),
            ],
        ),
        cost_estimate=pl.CostEstimate(
            flops=2 * 1280 * 256 * 256, bytes_accessed=2 * 2**20, transcendentals=0
        ),
        name="apply_last",
    )(place, mine, other, five, before)


def project_kernel(place, *refs):
    t_refs = refs[:8]
    mine, twin = refs[8:10]
    outs = refs[10:14]
    left, prol, sems = refs[14:]
    y, z, x, h, c = (place[i] for i in range(5))
    copies = []
    for i, k in enumerate(STEPS):
        m = lax.rem(x + 8 - k - y, 4)
        for f in range(2):
            src, dst = t_refs[4 * f + i], left.at[m, lax.rem(h + f, 2)]
            copy = pltpu.make_async_copy(src, dst, sems.at[2 * i + f])
            copy.start()
            copies.append(copy)
    prol[...] = jnp.where(c == lax.rem(z, 2), mine[...], twin[...])
    for copy in copies:
        copy.wait()
    for m in range(4):
        for k1 in range(2):
            total = jnp.zeros((128, 256), jnp.float32)
            for i in range(5):
                total += jnp.dot(
                    left[m, k1, pl.ds(i * 128, 128), :],
                    prol[pl.ds(i * 256, 256), :],
                    preferred_element_type=jnp.float32,
                )
            outs[m][pl.ds(k1 * 128, 128), :] = total


def project(place, t_pieces, mine, twin):
    anywhere = pl.BlockSpec(memory_space=pl.ANY)
    inside = pl.BlockSpec(memory_space=pltpu.VMEM)
    out = jax.ShapeDtypeStruct((256, 256), jnp.float32)
    return pl.pallas_call(
        project_kernel,
        out_shape=(out,) * 4,
        grid_spec=pltpu.PrefetchScalarGridSpec(
            num_scalar_prefetch=1,
            grid=(),
            in_specs=[anywhere] * 8 + [inside] * 2,
            out_specs=(inside,) * 4,
            scratch_shapes=[
                pltpu.VMEM((4, 2, 640, 256), jnp.bfloat16),
                pltpu.VMEM((1280, 256), jnp.bfloat16),
                pltpu.SemaphoreType.DMA((8,)),
            ],
        ),
        compiler_params=pltpu.CompilerParams(vmem_limit_bytes=32 * 2**20),
        cost_estimate=pl.CostEstimate(
            flops=2 * 1280 * 1024 * 256, bytes_accessed=4 * 2**20, transcendentals=0
        ),
        name="project",
    )(place, *t_pieces, mine, twin)


def per_device(a_vals, a_cols, a_count, p_vals, p_mask):
    row, col = lax.axis_index("row"), lax.axis_index("col")
    y, z = row // 4, row % 4
    x, h, c = col // 4, (col // 2) % 2, col % 2
    place = jnp.stack([y, z, x, h, c]).astype(jnp.int32)

    p_live = p_vals * p_mask[:, :, None].astype(jnp.bfloat16)
    p_flat = p_live.reshape(1280, 128)
    p_own = jnp.concatenate([p_flat, move(p_flat, flip_z1)])
    p_twin = move(p_own, flip_c)

    diagonal = (row == col).astype(jnp.int32).reshape(1)
    four, five = pack(a_count.reshape(20), diagonal, a_vals.reshape(20, 5, BR, BR), a_cols - col * 20)
    swapped = move(four, swap_zc)

    def across(y, z, x, h, c):
        return (y, z, x, 1 - h, c) if h == z // 2 and x == y and c == z % 2 else None

    def next_x(y, z, x, h, c):
        return (y, z, (x + 1) % 4, h, c) if x == y and c == z % 2 else None

    def over_x(y, z, x, h, c):
        return (y, z, (x + 2) % 4, h, c) if (x - y) % 4 < 2 and c == z % 2 else None


    p_own, near, four = after((p_own, swapped, four))
    far = move(four, cross_zc)
    a_near = [near] + [move(near, shift_x(k)) for k in (1, 3, 2)]
    p_mine = [p_own, move(p_own, shift_y(1))]
    far, p_own = after((far, p_own), *p_mine, *a_near)
    a_far = [far] + [move(far, shift_x(k)) for k in (1, 3, 2)]
    p_mine += [move(p_own, shift_y(k)) for k in (3, 2)]
    p_other = [p_twin] + [move(piece, flip_c) for piece in p_mine[1:]]

    t_own = p_flat.reshape(5, 256, 128).transpose(0, 2, 1).reshape(640, 256)
    t_own, five = after((t_own, five), *a_far, *p_other)
    t_far = move(t_own, flip_h)
    t_near = [t_own] + [move(t_own, shift_x(k)) for k in (1, 3, 2)]
    five = five + move(five, across)
    product = apply_panel(place, p_mine + p_other, a_near + a_far)
    product, t_far, five = after((product, t_far, five), *t_near)
    t_far = [t_far] + [move(t_far, shift_x(k)) for k in (1, 3, 2)]
    five = five + move(five, next_x)
    five = five + move(five, over_x)
    total = apply_last(place, p_mine[0], p_other[0], five, product)
    prolonged = (total + move(product, flip_z0)).astype(jnp.bfloat16)
    (prolonged,) = after((prolonged,), *t_near, *t_far)
    twin = move(prolonged, flip_c)

    blocks = project(place, t_near + t_far, prolonged, twin)
    summed = blocks[0]
    for m in (1, 2, 3):
        summed = summed + move(blocks[m], shift_y(m))
    parts = summed.reshape(2, 128, 2, 128)
    total = None
    for s in range(4):
        k1 = (z // 2 + s // 2) % 2
        l0 = (z + s) % 2
        part = lax.dynamic_slice(parts, (k1, 0, l0, 0), (1, 128, 1, 128)).reshape(128, 128)
        got = move(part, scatter_z(s))
        total = got if total is None else total + got
    return total


def solution(mesh):
    placed = (
        P("row", "col", None),
        P("row", "col"),
        P("row", "col"),
        P("row", None, "col"),
        P("row", "col"),
    )
    return jax.shard_map(
        per_device, mesh=mesh, in_specs=placed, out_specs=P("row", "col"), check_vma=False
    )
```
